256 devices in a mesh: blk: 32 (over y_lo, z, core), uly: 8 (over y_hi, x).
Axes of the slice: x: 4, y: 4 (y_hi: 2, y_lo: 2; y = y_hi * 2 + y_lo), z: 8, core: 2. Of those that a mesh axis runs over, the one named last changes fastest.
Arguments:
- video_tokens: bfloat16 [8192, 3072], P(('blk', 'uly')), may hold values from -6 to 6
- w_qkv: bfloat16 [3072, 9216], P(None, 'uly'), may hold values from -0.109375 to 0.109375
- w_out: bfloat16 [3072, 3072], P('uly'), may hold values from -0.109375 to 0.109375
- text_tokens: bfloat16 [256, 3072], P(None, 'blk'), may hold values from -6 to 6
- w_text: bfloat16 [3072, 6144], P('blk', 'uly'), may hold values from -0.109375 to 0.109375
- q_gain: float32 [128], replicated, may hold values from 1.5 to 5.5
- k_gain: float32 [128], replicated, may hold values from 1.5 to 5.5
- text_gain: float32 [128], replicated, may hold values from 1.5 to 5.5
Outputs:
- video_out: bfloat16 [8192, 3072], P(('blk', 'uly'))
The draws below stay inside these ranges and needn't reach their ends.
All inputs are finite; a program needn't handle non-finite values.
Results may differ from the reference program's by a relative error of at most 0.018.
The reference program's roundings to bfloat16 on the way (of `attended`) count: a program that leaves them out, or rounds other values in their place, can miss the bound.
Values may be sent and summed in bfloat16 or wider, within the bound.
A program may use at most 128 MiB of HBM per device.

```python
import jax
import jax.numpy as jnp
from jax import lax

D = 3072
HEADS = 24
HD = 128
TEXT = 256
BLOCK = 256
VIDEO = 8192


def gain_values(key, lowest, highest):
    spread = jax.random.uniform(key, (HD,), jnp.float32)
    return jnp.exp(jnp.log(lowest) + spread * (jnp.log(highest) - jnp.log(lowest)))


def draw_q_gain(key, part):
    key = jax.random.fold_in(key, 11)
    return gain_values(key, 1.6, 2.4)


def draw_k_gain(key, part):
    key = jax.random.fold_in(key, 12)
    return gain_values(key, 1.6, 2.4)


def draw_text_gain(key, part):
    key = jax.random.fold_in(key, 13)
    return gain_values(key, 1.6, 2.4)


def levels(key, dims, cuts, low, largest):
    level = 1.0
    for axis_at, blocks in cuts:
        heights = jax.random.uniform(jax.random.fold_in(jax.random.fold_in(key, 6), axis_at), (blocks,), jnp.float32, low / len(cuts), largest / len(cuts))
        level = level * jnp.repeat(jnp.exp(heights), dims[axis_at] // blocks).reshape((-1,) + (1,) * (len(dims) - 1 - axis_at))
    return level


def bell_draw(rng, shape, width, most, pieces=(), kind=jnp.bfloat16):
    array = width * jax.random.normal(rng, shape, jnp.float32)
    if pieces:
        array = array * levels(rng, shape, pieces, -0.22, 0.18)
    return jnp.clip(array, -most, most).astype(kind)


def setup_inputs(seed: int = 0) -> dict:
    seeds = jax.random.split(jax.random.key(seed), 9)
    video_tokens = bell_draw(seeds[0], (VIDEO, D), 1.0, 6.0, ((0, 256),))
    w_qkv = bell_draw(seeds[1], (D, 3 * D), D ** -0.5, 0.109375, ((1, 8),))
    w_out = bell_draw(seeds[2], (D, D), D ** -0.5, 0.109375, ((0, 8),))
    text_tokens = bell_draw(seeds[3], (TEXT, D), 1.0, 6.0, ((1, 32),))
    w_text = bell_draw(seeds[4], (D, 2 * D), D ** -0.5, 0.109375, ((0, 32), (1, 8)))
    q_gain = draw_q_gain(jax.random.fold_in(seeds[8], 71), 0)
    k_gain = draw_k_gain(jax.random.fold_in(seeds[8], 71), 0)
    text_gain = draw_text_gain(jax.random.fold_in(seeds[8], 71), 0)
    return {"video_tokens": video_tokens, "w_qkv": w_qkv, "w_out": w_out, "text_tokens": text_tokens, "w_text": w_text, "q_gain": q_gain, "k_gain": k_gain, "text_gain": text_gain}


def normed(values, gains):
    factor = lax.rsqrt(lax.optimization_barrier(jnp.mean(values * values, axis=-1, keepdims=True)) + 1e-06)
    return values * factor * gains

def reference(video_tokens, w_qkv, w_out, text_tokens, w_text, q_gain, k_gain, text_gain):
    projected = jnp.dot(video_tokens, w_qkv, preferred_element_type=jnp.float32).reshape(VIDEO, HEADS, 3, HD)
    queries = normed(projected[:, :, 0], q_gain).astype(jnp.bfloat16)
    video_keys = normed(projected[:, :, 1], k_gain).astype(jnp.bfloat16)
    video_values = projected[:, :, 2].astype(jnp.bfloat16)
    text_projected = jnp.dot(text_tokens, w_text, preferred_element_type=jnp.float32).reshape(TEXT, HEADS, 2, HD)
    text_keys = normed(text_projected[:, :, 0], text_gain).astype(jnp.bfloat16)
    text_values = text_projected[:, :, 1].astype(jnp.bfloat16)
    all_keys = jnp.concatenate([text_keys, video_keys], axis=0)
    all_values = jnp.concatenate([text_values, video_values], axis=0)
    score_scale = HD ** (-0.5)

    def one_head(head_index):
        head_keys = lax.dynamic_index_in_dim(all_keys, head_index, 1, keepdims=False)
        head_values = lax.dynamic_index_in_dim(all_values, head_index, 1, keepdims=False)
        head_queries = lax.dynamic_index_in_dim(queries, head_index, 1, keepdims=False)
        head_queries = head_queries.reshape(VIDEO // BLOCK, BLOCK, HD)

        def one_block(block_queries):
            scores = jnp.dot(block_queries, head_keys.T, preferred_element_type=jnp.float32) * score_scale
            row_peak = lax.optimization_barrier(jnp.max(scores, axis=-1, keepdims=True))
            weights = jnp.exp(scores - row_peak)
            row_total = lax.optimization_barrier(jnp.sum(weights, axis=-1, keepdims=True))
            blended = jnp.dot(weights.astype(jnp.bfloat16), head_values, preferred_element_type=jnp.float32)
            return (blended / row_total).astype(jnp.bfloat16)
        return lax.map(one_block, head_queries).reshape(VIDEO, HD)
    heads_out = lax.map(one_head, jnp.arange(HEADS, dtype=jnp.int32))
    attended = jnp.transpose(heads_out, (1, 0, 2)).reshape(VIDEO, D)
    return jnp.dot(attended, w_out, preferred_element_type=jnp.float32).astype(jnp.bfloat16)
```

```python
import functools
import math

import jax
import jax.numpy as jnp
from jax import lax
from jax.experimental import pallas as pl
from jax.experimental.pallas import tpu as pltpu
from jax.sharding import PartitionSpec as P

MESH = pl.DeviceIdType.MESH
HD = 128
NH = 3
D = 3072
TEXT = 256
ROWS = 32
HALF = 16
CHUNK = 128
NZ, NX = 8, 4
SCALE2 = HD ** (-0.5) * math.log2(math.e)
BF16, F32 = jnp.bfloat16, jnp.float32


class Sems:
    def __init__(self, send, recv):
        self.send, self.recv, self.at = send, recv, {}

    def __call__(self, *name):
        index = self.at.setdefault(name, len(self.at))
        return {"send_sem": self.send.at[index], "recv_sem": self.recv.at[index]}


N_SEMS = 96


def normed(values, gains):
    factor = lax.rsqrt(jnp.mean(values * values, axis=-1, keepdims=True) + 1e-06)
    return values * factor * gains


def kernel(
    tok_hbm, wq_hbm, wo_hbm, tt_ref, wt_ref, qg_ref, kg_ref, tg_ref, out_ref,
    tok, relay, wq, wo, kv, q, acc, top, total,
    tpart, tcr, tsum, tyr, tsum2, tzr, tkv,
    osend, orecv, ssend, srecv, part, rsrecv,
    send_sems, recv_sems, local_sems,
):
    b, u = lax.axis_index("blk"), lax.axis_index("uly")
    y_lo, z, c = b // 16, (b // 2) % NZ, b % 2
    y_hi, x = u // NX, u % NX
    y = 2 * y_hi + y_lo
    sems = Sems(send_sems, recv_sems)
    pending = []

    def device(y_lo=y_lo, z=z, c=c, y_hi=y_hi, x=x):
        return {"blk": (y_lo * NZ + z) * 2 + c, "uly": y_hi * NX + x}

    def y_step(k):
        yy = (y + k) % 4
        return device(y_hi=yy // 2, y_lo=yy % 2)

    def x_step(k):
        return device(x=(x + k) % NX)

    def z_step(k):
        return device(z=(z + k) % NZ)

    sibling = device(c=1 - c)
    partner = device(y_lo=1 - y_lo)

    def send(name, src, dst, where):
        copy = pltpu.make_async_remote_copy(
            src_ref=src, dst_ref=dst, device_id=where, device_id_type=MESH, **sems(*name)
        )
        copy.start()
        pending.append(copy)

    def wait(name, dst):
        pltpu.make_async_remote_copy(
            src_ref=dst, dst_ref=dst, device_id=sibling, device_id_type=MESH, **sems(*name)
        ).wait_recv()

    barrier = pltpu.get_barrier_semaphore()
    peers = [device(z=(z + dz) % NZ, c=(c + dc) % 2) for dz in range(NZ) for dc in range(2) if dz or dc]
    peers += [y_step(1), y_step(-1)]
    peers += [device(y_hi=(y_hi + j) % 2, x=(x + dx) % NX) for j in range(2) for dx in range(NX) if j or dx]
    for peer in peers:
        pl.semaphore_signal(barrier, inc=1, device_id=peer, device_id_type=MESH)
    pl.semaphore_wait(barrier, len(peers))

    def rows(start, size, step):
        return pl.ds(pl.multiple_of(start * step, step), size)

    def slot(j, dx, first=0, size=ROWS):
        start = ((x + dx) % NX) * ROWS + first
        return tok.at[(y_hi + j) % 2, pl.ds(pl.multiple_of(start, HALF), size), :]

    local_tok = pltpu.make_async_copy(tok_hbm, slot(0, 0), local_sems.at[0])
    local_wq = pltpu.make_async_copy(wq_hbm, wq, local_sems.at[1])
    local_wo = pltpu.make_async_copy(wo_hbm, wo, local_sems.at[2])

    send(("x", 0, 1), tok_hbm, slot(0, 0), x_step(1))
    send(("x", 0, -1), tok_hbm, slot(0, 0), x_step(-1))
    for k, first in ((1, 0), (-1, HALF)):
        send(("y", k), tok_hbm.at[pl.ds(first, HALF), :], relay.at[first // HALF], y_step(k))
    local_tok.start()
    local_wq.start()
    local_wo.start()

    product = jnp.dot(tt_ref[...], wt_ref[...], preferred_element_type=F32)
    for h in range(NH):
        for s in range(2):
            at = (2 * h + s) * HD
            tpart[s, :, h * HD:(h + 1) * HD] = product[:, at:at + HD]
    send(("tc",), tpart.at[1 - c], tcr, sibling)

    for k, first in ((1, 0), (-1, HALF)):
        wait(("y", k), relay.at[first // HALF])
        source = (y - k) % 4
        dst = tok.at[source // 2, pl.ds(pl.multiple_of(x * ROWS + first, HALF), HALF), :]
        send(("yy", k), relay.at[first // HALF], dst, y_step(k))

    def pass_on(j):
        for k, first in ((1, 0), (-1, HALF)):
            wait(("x", j, k), slot(j, -k))
            send(("xx", j, k), slot(j, -k, first, HALF), slot(j, -k, first, HALF), x_step(k))

    pass_on(0)

    wait(("tc",), tcr)
    tsum[...] = tpart[c] + tcr[...]
    send(("ty",), tsum.at[rows(1 - y_lo, CHUNK, CHUNK), :], tyr, partner)

    for k, first in ((1, 0), (-1, HALF)):
        wait(("yy", k), slot(1, 0, first, HALF))
    send(("x", 1, 1), slot(1, 0), slot(1, 0), x_step(1))
    send(("x", 1, -1), slot(1, 0), slot(1, 0), x_step(-1))

    def project(j):
        for k, first in ((1, 0), (-1, HALF)):
            wait(("xx", j, k), slot(j, 2, first, HALF))
        mine = rows(c, CHUNK, CHUNK)

        @pl.loop(0, NH)
        def _(h):
            columns = pl.ds(pl.multiple_of(h * 3 * HD, HD), 3 * HD)
            r = jnp.dot(tok[(y_hi + j) % 2], wq[:, columns], preferred_element_type=F32)
            q[h, j * CHUNK:(j + 1) * CHUNK, :] = normed(r[:, :HD], qg_ref[...]).astype(BF16)
            kv[j, z, h, mine, :] = normed(r[:, HD:2 * HD], kg_ref[...]).astype(BF16)
            kv[j, z, NH + h, mine, :] = r[:, 2 * HD:].astype(BF16)

        block = kv.at[j, z, :, mine, :]
        send(("kv", j, 1, 1), block, block, z_step(1))
        send(("kv", j, -1, 1), block, block, z_step(-1))
        send(("sib", j, 0, 0), block, block, sibling)
        own, theirs = j * CHUNK, 2 * CHUNK + j * CHUNK
        send(("q", j), q.at[:, own:own + CHUNK, :], q.at[:, theirs:theirs + CHUNK, :], partner)

    def planes(h, k):
        if h < NZ // 2:
            return pl.ds(0, 2 * NH)
        return pl.ds(0 if k == 1 else NH, NH)

    def block_of(j, h, k, p, core):
        return kv.at[j, (z - k * h) % NZ, p, rows(core, CHUNK, CHUNK), :]

    def ring(j, h):
        for k in (1, -1):
            wait(("kv", j, k, h), block_of(j, h, k, planes(h, k), c))
            if h < NZ // 2:
                piece = block_of(j, h, k, planes(h + 1, k), c)
                send(("kv", j, k, h + 1), piece, piece, z_step(k))
        for k in (1, -1):
            piece = block_of(j, h, k, planes(h, k), c)
            send(("sib", j, h, k), piece, piece, sibling)

    def await_sibling(j, h):
        for k in (1, -1) if h else (0,):
            wait(("sib", j, h, k), block_of(j, h, k, planes(h, k) if h else pl.ds(0, 2 * NH), 1 - c))

    def attend(tiles):
        @pl.loop(0, 2)
        def _(t):
            at = rows(t, 2 * CHUNK, 2 * CHUNK)
            for h in range(NH):
                pairs = tiles(h)
                scores = []
                for keys, _ in pairs:
                    s = lax.dot_general(q[h, at, :], keys[...], (((1,), (1,)), ((), ())), preferred_element_type=F32)
                    scores.append([s[:, i:i + HD] for i in range(0, s.shape[1], HD)])
                peak = functools.reduce(jnp.maximum, [piece for s in scores for piece in s])
                old = top[h, at, :]
                new = jnp.maximum(old, jnp.max(peak, axis=1, keepdims=True))
                shrink = jnp.exp2((old - new) * SCALE2)
                weights = [[jnp.exp2((piece - new) * SCALE2) for piece in s] for s in scores]
                total[h, at, :] = total[h, at, :] * shrink + sum(piece for w in weights for piece in w)
                blended = acc[h, at, :] * shrink
                for w, (_, values) in zip(weights, pairs):
                    w = jnp.concatenate(w, axis=1).astype(BF16)
                    blended = blended + jnp.dot(w, values[...], preferred_element_type=F32)
                acc[h, at, :] = blended
                top[h, at, :] = new

    def video_tiles(*where):
        def tiles(h):
            return [(kv.at[j, zz, h], kv.at[j, zz, NH + h]) for j, zz in where]

        return tiles

    local_tok.wait()
    local_wq.wait()
    project(0)

    wait(("ty",), tyr)
    tsum2[...] = tsum[rows(y_lo, CHUNK, CHUNK), :] + tyr[...]
    for dz in range(1, NZ):
        target = (z + dz) % NZ
        send(("tz", dz), tsum2.at[rows(target, HALF, HALF), :], tzr.at[dz - 1], z_step(dz))

    pass_on(1)

    top[...] = jnp.full(top.shape, -1e30, F32)
    total[...] = jnp.zeros(total.shape, F32)
    acc[...] = jnp.zeros(acc.shape, F32)

    ring(0, 1)
    project(1)

    for dz in range(1, NZ):
        wait(("tz", dz), tzr.at[dz - 1])
    summed = tsum2[rows(z, HALF, HALF), :]
    for dz in range(1, NZ):
        summed = summed + tzr[dz - 1]
    for h in range(NH):
        one = summed[:, h * HD:(h + 1) * HD]
        one = jnp.where(c == 0, normed(one, tg_ref[...]), one)
        tkv[c * NH + h, rows(z, HALF, HALF), :] = one.astype(BF16)

    def text_piece(dz, dc):
        return tkv.at[pl.ds(((c + dc) % 2) * NH, NH), rows((z - dz) % NZ, HALF, HALF), :]

    others = [(dz, dc) for dz in range(NZ) for dc in range(2) if dz or dc]
    for dz, dc in others:
        send(("tg", dz, dc), text_piece(0, 0), text_piece(0, 0), device(z=(z + dz) % NZ, c=(c + dc) % 2))

    for j in range(2):
        theirs = 2 * CHUNK + j * CHUNK
        wait(("q", j), q.at[:, theirs:theirs + CHUNK, :])
    await_sibling(0, 0)
    await_sibling(1, 0)
    attend(video_tiles((0, z), (1, z)))

    def attend_far(j, h):
        await_sibling(j, h)
        attend(video_tiles((j, (z - h) % NZ), (j, (z + h) % NZ)))

    ring(1, 1)
    attend_far(0, 1)
    ring(0, 2)
    attend_far(1, 1)
    ring(1, 2)
    attend_far(0, 2)
    ring(0, 3)
    attend_far(1, 2)
    ring(1, 3)
    for dz, dc in others:
        wait(("tg", dz, dc), text_piece(dz, dc))
    attend(lambda h: [(tkv.at[h], tkv.at[NH + h])])
    attend_far(0, 3)
    ring(0, 4)
    attend_far(1, 3)
    ring(1, 4)
    await_sibling(0, 4)
    await_sibling(1, 4)
    attend(video_tiles((0, (z + 4) % NZ), (1, (z + 4) % NZ)))

    def finished(h, at):
        weight = jnp.sum(total[h, at, :], axis=1, keepdims=True)
        return acc[h, at, :] / weight, top[h, at, :] * SCALE2 + jnp.log2(weight)

    ssend[...] = jnp.zeros(ssend.shape, F32)
    for j in (1, 0):
        for h in range(NH):
            mean, level = finished(h, pl.ds(2 * CHUNK + j * CHUNK, CHUNK))
            osend[j, :, h * HD:(h + 1) * HD] = mean.astype(BF16)
            ssend[j, h:h + 1, :] = level.T[0:1, :]
        send(("s", j), ssend.at[j], srecv.at[j], partner)
        send(("o", j), osend.at[j], orecv.at[j], partner)

    local_wo.wait()
    for j in (1, 0):
        wait(("s", j), srecv.at[j])
        wait(("o", j), orecv.at[j])
        mixed = []
        for h in range(NH):
            mean, level = finished(h, pl.ds(j * CHUNK, CHUNK))
            other = jnp.broadcast_to(srecv[j, h:h + 1, :], (CHUNK, HD)).T
            peak = jnp.maximum(level, other)
            mine, theirs = jnp.exp2(level - peak), jnp.exp2(other - peak)
            both = mean * mine + orecv[j, :, h * HD:(h + 1) * HD].astype(F32) * theirs
            mixed.append((both / (mine + theirs)).astype(BF16))
        attended = jnp.concatenate(mixed, axis=1)
        for n in range(0, D, 512):
            r = jnp.dot(attended, wo[:, n:n + 512], preferred_element_type=F32)
            part[j, :, n:n + 512] = r.astype(BF16)
        for dx in (2, 1, 3, 0):
            if j or dx:
                where = device(y_hi=(y_hi + j) % 2, x=(x + dx) % NX)
                src = part.at[j, rows((x + dx) % NX, ROWS, ROWS), :]
                send(("rs", j, dx), src, rsrecv.at[j * NX + dx - 1], where)

    for j in (0, 1):
        for dx in range(NX):
            if j or dx:
                wait(("rs", j, dx), rsrecv.at[j * NX + dx - 1])

    for n in range(0, D, 512):
        out = part[0, rows(x, ROWS, ROWS), n:n + 512].astype(F32)
        for i in range(2 * NX - 1):
            out = out + rsrecv[i, :, n:n + 512].astype(F32)
        out_ref[:, n:n + 512] = out.astype(BF16)

    for copy in pending:
        copy.wait_send()


def per_device(video_tokens, w_qkv, w_out, text_tokens, w_text, q_gain, k_gain, text_gain):
    vmem, hbm = pl.BlockSpec(memory_space=pltpu.VMEM), pl.BlockSpec(memory_space=pl.ANY)
    return pl.pallas_call(
        kernel,
        out_shape=jax.ShapeDtypeStruct((ROWS, D), BF16),
        in_specs=[hbm, hbm, hbm] + [vmem] * 5,
        out_specs=vmem,
        scratch_shapes=[
            pltpu.VMEM((2, CHUNK, D), BF16),
            pltpu.VMEM((2, HALF, D), BF16),
            pltpu.VMEM((D, NH * 3 * HD), BF16),
            pltpu.VMEM((NH * HD, D), BF16),
            pltpu.VMEM((2, NZ, 2 * NH, 2 * CHUNK, HD), BF16),
            pltpu.VMEM((NH, 4 * CHUNK, HD), BF16),
            pltpu.VMEM((NH, 4 * CHUNK, HD), F32),
            pltpu.VMEM((NH, 4 * CHUNK, HD), F32),
            pltpu.VMEM((NH, 4 * CHUNK, HD), F32),
            pltpu.VMEM((2, TEXT, NH * HD), F32),
            pltpu.VMEM((TEXT, NH * HD), F32),
            pltpu.VMEM((TEXT, NH * HD), F32),
            pltpu.VMEM((CHUNK, NH * HD), F32),
            pltpu.VMEM((CHUNK, NH * HD), F32),
            pltpu.VMEM((NZ - 1, HALF, NH * HD), F32),
            pltpu.VMEM((2 * NH, CHUNK, HD), BF16),
            pltpu.VMEM((2, CHUNK, NH * HD), BF16),
            pltpu.VMEM((2, CHUNK, NH * HD), BF16),
            pltpu.VMEM((2, 8, HD), F32),
            pltpu.VMEM((2, 8, HD), F32),
            pltpu.VMEM((2, CHUNK, D), BF16),
            pltpu.VMEM((2 * NX - 1, ROWS, D), BF16),
            pltpu.SemaphoreType.DMA((N_SEMS,)),
            pltpu.SemaphoreType.DMA((N_SEMS,)),
            pltpu.SemaphoreType.DMA((3,)),
        ],
        compiler_params=pltpu.CompilerParams(
            collective_id=0, has_side_effects=True, vmem_limit_bytes=56 * 1024 * 1024
        ),
        name="joint_attention",
    )(
        video_tokens, w_qkv, w_out, text_tokens, w_text,
        q_gain.reshape(1, HD), k_gain.reshape(1, HD), text_gain.reshape(1, HD),
    )


def solution(mesh):
    in_specs = (
        P(("blk", "uly"), None), P(None, "uly"), P("uly", None), P(None, "blk"), P("blk", "uly"), P(), P(), P(),
    )
    return jax.shard_map(
        per_device, mesh=mesh, in_specs=in_specs, out_specs=P(("blk", "uly"), None), check_vma=False
    )
```

```python
import functools
import math

import jax
import jax.numpy as jnp
from jax import lax
from jax.experimental import pallas as pl
from jax.experimental.pallas import tpu as pltpu
from jax.sharding import PartitionSpec as P

MESH = pl.DeviceIdType.MESH
HD = 128
NH = 3
D = 3072
TEXT = 256
ROWS = 32
HALF = 16
CHUNK = 128
NZ, NX = 8, 4
COLS = D // 2
SHARE = NH * HD // 2
SLOTS = ((0, 0), (1, 0), (-1, 0), (0, 1), (2, 0), (1, 1), (-1, 1), (2, 1))
SLOT = {where: s for s, where in enumerate(SLOTS)}
POS = {0: 0, 1: 1, -1: 2, 2: 3}
GROUPS = ((0, 1), (1, 3), (4, 1), (5, 2), (7, 1))
SCALE2 = HD ** (-0.5) * math.log2(math.e)
BF16, F32 = jnp.bfloat16, jnp.float32


class Sems:
    def __init__(self, send, recv):
        self.send, self.recv, self.at = send, recv, {}

    def __call__(self, *name):
        index = self.at.setdefault(name, len(self.at))
        return {"send_sem": self.send.at[index], "recv_sem": self.recv.at[index]}


N_SEMS = 128


def normed(values, gains):
    factor = lax.rsqrt(jnp.mean(values * values, axis=-1, keepdims=True) + 1e-06)
    return values * factor * gains


def kernel(
    tok_hbm, wq_hbm, wo_hbm, tt_ref, wt_ref, qg_ref, kg_ref, tg_ref, out_ref,
    tok, wq, wo, kv, q, acc, top, total,
    tpart, tcr, tsum, tyr, tsum2, tzr, tkv,
    osend, orecv, ssend, srecv, att, arecv, part, precv,
    send_sems, recv_sems, local_sems,
):
    b, u = lax.axis_index("blk"), lax.axis_index("uly")
    y_lo, z, c = b // 16, (b // 2) % NZ, b % 2
    y_hi, x = u // NX, u % NX
    y = 2 * y_hi + y_lo
    sems = Sems(send_sems, recv_sems)
    pending = []

    def device(y_lo=y_lo, z=z, c=c, y_hi=y_hi, x=x):
        return {"blk": (y_lo * NZ + z) * 2 + c, "uly": y_hi * NX + x}

    def y_step(k):
        yy = (y + k) % 4
        return device(y_hi=yy // 2, y_lo=yy % 2)

    def x_step(k, o=0):
        return device(x=(x + k) % NX, y_lo=(y_lo + o) % 2)

    def z_step(k):
        return device(z=(z + k) % NZ)

    sibling = device(c=1 - c)
    partner = device(y_lo=1 - y_lo)

    def send(name, src, dst, where):
        copy = pltpu.make_async_remote_copy(
            src_ref=src, dst_ref=dst, device_id=where, device_id_type=MESH, **sems(*name)
        )
        copy.start()
        pending.append(copy)

    def wait(name, dst):
        pltpu.make_async_remote_copy(
            src_ref=dst, dst_ref=dst, device_id=sibling, device_id_type=MESH, **sems(*name)
        ).wait_recv()

    barrier = pltpu.get_barrier_semaphore()
    peers = [x_step(k, o) for k in (1, -1, 2) for o in range(2)]
    peers += [y_step(k) for k in (1, -1, 2)]
    peers += [z_step(k) for k in range(1, NZ)] + [sibling]
    for peer in peers:
        pl.semaphore_signal(barrier, inc=1, device_id=peer, device_id_type=MESH)

    def rows(start, size, step):
        return pl.ds(pl.multiple_of(start * step, step), size)

    def slot(dx, dy):
        return tok.at[SLOT[dx, dy]]

    mine = rows(y_lo, COLS, COLS)
    local_tok = pltpu.make_async_copy(tok_hbm, slot(0, 0), local_sems.at[0])
    local_wq = pltpu.make_async_copy(wq_hbm, wq, local_sems.at[1])
    local_wo = pltpu.make_async_copy(wo_hbm.at[:, mine], wo.at[0], local_sems.at[2])
    local_tok.start()
    local_wq.start()

    product = lax.dot_general(tt_ref[...], wt_ref[...], (((0,), (0,)), ((), ())), preferred_element_type=F32)
    for h in range(NH):
        for s in range(2):
            at = (2 * h + s) * HD
            tpart[s, :, h * HD:(h + 1) * HD] = product[:, at:at + HD]
    top[...] = jnp.full(top.shape, -1e30, F32)
    total[...] = jnp.zeros(total.shape, F32)
    acc[...] = jnp.zeros(acc.shape, F32)
    ssend[...] = jnp.zeros(ssend.shape, F32)

    def kv_rows(g, core):
        first, count = GROUPS[g]
        return pl.ds(pl.multiple_of(core * CHUNK + first % 4 * ROWS, ROWS), count * ROWS)

    def project(g):
        first, count = GROUPS[g]
        j = first // 4

        @pl.loop(0, NH)
        def _(h):
            columns = pl.ds(pl.multiple_of(h * 3 * HD, HD), 3 * HD)
            left = tok[first:first + count].reshape(count * ROWS, D)
            r = jnp.dot(left, wq[:, columns], preferred_element_type=F32)
            q[h, first * ROWS:(first + count) * ROWS, :] = normed(r[:, :HD], qg_ref[...]).astype(BF16)
            kv[j, z, h, kv_rows(g, c), :] = normed(r[:, HD:2 * HD], kg_ref[...]).astype(BF16)
            kv[j, z, NH + h, kv_rows(g, c), :] = r[:, 2 * HD:].astype(BF16)

    def ring_start(g):
        block = kv.at[GROUPS[g][0] // 4, z, :, kv_rows(g, c), :]
        for k in (1, -1):
            send(("kv", g, k, 1), block, block, z_step(k))

    def finish_chunk(j):
        block = kv.at[j, z, :, rows(c, CHUNK, CHUNK), :]
        send(("sib", j, 0, 0), block, block, sibling)
        own, theirs = j * CHUNK, 2 * CHUNK + j * CHUNK
        send(("q", j), q.at[:, own:own + CHUNK, :], q.at[:, theirs:theirs + CHUNK, :], partner)

    def planes(h, k):
        if h < NZ // 2:
            return pl.ds(0, 2 * NH)
        return pl.ds(0 if k == 1 else NH, NH)

    def ring(g, h):
        j = GROUPS[g][0] // 4
        for k in (1, -1):
            zz = (z - k * h) % NZ
            wait(("kv", g, k, h), kv.at[j, zz, planes(h, k), kv_rows(g, c), :])
            if h < NZ // 2:
                piece = kv.at[j, zz, planes(h + 1, k), kv_rows(g, c), :]
                send(("kv", g, k, h + 1), piece, piece, z_step(k))

    def share(j, h):
        for k in (1, -1):
            piece = kv.at[j, (z - k * h) % NZ, planes(h, k), rows(c, CHUNK, CHUNK), :]
            send(("sib", j, h, k), piece, piece, sibling)

    def await_sibling(j, h):
        for k in (1, -1) if h else (0,):
            piece = planes(h, k) if h else pl.ds(0, 2 * NH)
            wait(("sib", j, h, k), kv.at[j, (z - k * h) % NZ, piece, rows(1 - c, CHUNK, CHUNK), :])

    def attend(tiles, first=0, size=4 * CHUNK):
        at = pl.ds(first, size)
        for h in range(NH):
            pairs = tiles(h)
            scores = []
            for keys, _ in pairs:
                s = lax.dot_general(q[h, at, :], keys[...], (((1,), (1,)), ((), ())), preferred_element_type=F32)
                scores.append([s[:, i:i + HD] for i in range(0, s.shape[1], HD)])
            peak = functools.reduce(jnp.maximum, [piece for s in scores for piece in s])
            old = top[h, at, :]
            new = jnp.maximum(old, jnp.max(peak, axis=1, keepdims=True))
            shrink = jnp.exp2((old - new) * SCALE2)
            weights = [[jnp.exp2((piece - new) * SCALE2) for piece in s] for s in scores]
            total[h, at, :] = total[h, at, :] * shrink + sum(piece for w in weights for piece in w)
            blended = acc[h, at, :] * shrink
            for w, (_, values) in zip(weights, pairs):
                w = jnp.concatenate(w, axis=1).astype(BF16)
                blended = blended + jnp.dot(w, values[...], preferred_element_type=F32)
            acc[h, at, :] = blended
            top[h, at, :] = new

    def video_tiles(*where):
        def tiles(h):
            return [(kv.at[j, zz, h], kv.at[j, zz, NH + h]) for j, zz in where]

        return tiles

    local_tok.wait()
    local_wq.wait()
    local_wo.start()
    project(0)

    pl.semaphore_wait(barrier, len(peers))

    for k in (1, -1):
        send(("x", k), tok_hbm, slot(-k, 0), x_step(k))
    send(("y",), tok_hbm, slot(0, 1), y_step(2))
    ring_start(0)
    send(("tc",), tpart.at[1 - c], tcr, sibling)
    ring(0, 1)
    send(("x", 2), tok_hbm, slot(2, 0), x_step(2))

    wait(("tc",), tcr)
    tsum[...] = tpart[c] + tcr[...]
    send(("ty",), tsum.at[rows(1 - y_lo, CHUNK, CHUNK), :], tyr, partner)

    wait(("y",), slot(0, 1))
    for k in (1, -1):
        send(("yx", k), slot(0, 1), slot(-k, 1), x_step(k))
    for k in (1, -1):
        wait(("x", k), slot(-k, 0))
    project(1)
    ring_start(1)
    finish_chunk(0)
    ring(0, 2)
    wait(("x", 2), slot(2, 0))
    send(("xy",), slot(2, 0), slot(2, 1), y_step(2))
    project(2)
    ring_start(2)

    ring(0, 3)
    ring(1, 1)
    share(0, 1)
    for k in (1, -1):
        wait(("yx", k), slot(-k, 1))

    project(3)
    ring_start(3)

    for k in (1, -1):
        here = rows(c, SHARE, SHARE)
        send(("w", k), wo_hbm.at[here, mine], wo.at[POS[-k], here, :], x_step(k))
    ring(0, 4)
    ring(2, 1)

    wait(("ty",), tyr)
    tsum2[...] = tsum[rows(y_lo, CHUNK, CHUNK), :] + tyr[...]
    for dz in range(1, NZ):
        target = (z + dz) % NZ
        send(("tz", dz), tsum2.at[rows(target, HALF, HALF), :], tzr.at[dz - 1], z_step(dz))

    wait(("xy",), slot(2, 1))
    project(4)
    ring_start(4)
    finish_chunk(1)

    ring(1, 2)
    share(0, 2)
    ring(2, 2)

    for dz in range(1, NZ):
        wait(("tz", dz), tzr.at[dz - 1])
    summed = tsum2[rows(z, HALF, HALF), :]
    for dz in range(1, NZ):
        summed = summed + tzr[dz - 1]
    for h in range(NH):
        one = summed[:, h * HD:(h + 1) * HD]
        one = jnp.where(c == 0, normed(one, tg_ref[...]), one)
        tkv[c * NH + h, rows(z, HALF, HALF), :] = one.astype(BF16)

    def text_piece(dz):
        return tkv.at[pl.ds(c * NH, NH), rows((z - dz) % NZ, HALF, HALF), :]

    for dz in range(1, NZ):
        send(("tg", dz), text_piece(0), text_piece(0), z_step(dz))

    for j in range(2):
        theirs = 2 * CHUNK + j * CHUNK
        wait(("q", j), q.at[:, theirs:theirs + CHUNK, :])
    await_sibling(0, 0)
    await_sibling(1, 0)
    attend(video_tiles((0, z), (1, z)))

    def attend_far(j, h):
        await_sibling(j, h)
        attend(video_tiles((j, (z - h) % NZ), (j, (z + h) % NZ)))

    ring(3, 1)
    ring(4, 1)
    share(1, 1)
    attend_far(0, 1)
    ring(2, 3)
    ring(1, 3)
    share(0, 3)
    attend_far(0, 2)
    ring(3, 2)
    ring(4, 2)
    share(1, 2)
    attend_far(1, 1)
    ring(2, 4)
    ring(1, 4)
    share(0, 4)
    attend_far(0, 3)
    for dz in range(1, NZ):
        wait(("tg", dz), text_piece(dz))
    text_half = tkv.at[pl.ds(c * NH, NH), :, :]
    send(("ts",), text_half, text_half, sibling)

    def w_piece(dx, first=0, size=SHARE):
        return wo.at[POS[dx], pl.ds(pl.multiple_of(c * SHARE + first, SHARE // 2), size), :]

    for k, first in ((1, 0), (-1, SHARE // 2)):
        wait(("w", k), w_piece(-k))
        send(("ww", k), w_piece(-k, first, SHARE // 2), w_piece(2, first, SHARE // 2), x_step(k))
        send(("ws", -k), w_piece(-k), w_piece(-k), sibling)

    attend_far(1, 2)
    ring(3, 3)
    ring(4, 3)
    share(1, 3)
    wait(("ts",), tkv.at[pl.ds((1 - c) * NH, NH), :, :])
    attend(lambda h: [(tkv.at[h], tkv.at[NH + h])])
    await_sibling(0, 4)
    attend(video_tiles((0, (z + 4) % NZ)))
    attend_far(1, 3)
    ring(3, 4)
    ring(4, 4)
    share(1, 4)
    await_sibling(1, 4)
    last = video_tiles((1, (z + 4) % NZ))
    attend(last, 2 * CHUNK, 2 * CHUNK)

    def finished(h, at):
        weight = jnp.sum(total[h, at, :], axis=1, keepdims=True)
        return acc[h, at, :] / weight, top[h, at, :] * SCALE2 + jnp.log2(weight)

    for j in (1, 0):
        for h in range(NH):
            mean, level = finished(h, pl.ds(2 * CHUNK + j * CHUNK, CHUNK))
            osend[j, :, h * HD:(h + 1) * HD] = mean.astype(BF16)
            ssend[j, h:h + 1, :] = level.T[0:1, :]
        send(("s", j), ssend.at[j], srecv.at[j], partner)
        send(("o", j), osend.at[j], orecv.at[j], partner)

    attend(last, 0, 2 * CHUNK)

    while len(pending) > 4:
        pending.pop(0).wait_send()
    for k, first in ((1, 0), (-1, SHARE // 2)):
        wait(("ww", k), w_piece(2, first, SHARE // 2))
    send(("ws", 2), w_piece(2), w_piece(2), sibling)

    for j in (1, 0):
        wait(("s", j), srecv.at[j])
        wait(("o", j), orecv.at[j])
        for h in range(NH):
            mean, level = finished(h, pl.ds(j * CHUNK, CHUNK))
            other = jnp.broadcast_to(srecv[j, h:h + 1, :], (CHUNK, HD)).T
            peak = jnp.maximum(level, other)
            ours, theirs = jnp.exp2(level - peak), jnp.exp2(other - peak)
            both = mean * ours + orecv[j, :, h * HD:(h + 1) * HD].astype(F32) * theirs
            both = (both / (ours + theirs)).astype(BF16)
            for i in range(4):
                dx, dy = SLOTS[4 * j + i]
                att[POS[dx], dy, :, h * HD:(h + 1) * HD] = both[i * ROWS:(i + 1) * ROWS]

        for o in (1, 0):
            if j == 1:
                send(("a", 2, o), att.at[POS[2]], arecv.at[POS[2], o], x_step(2, o))
            for k in (1, -1):
                send(("a", -k, o, j), att.at[POS[k], j], arecv.at[POS[-k], o, j], x_step(k, o))
            if j == 0 and o == 1:
                send(("a", 0, o), att.at[0], arecv.at[0, o], partner)

    arecv[0, 0] = att[0]

    local_wo.wait()
    for dx in (1, -1, 2):
        wait(("ws", dx), wo.at[POS[dx], rows(1 - c, SHARE, SHARE), :])
    for o in range(2):
        for k in (1, -1):
            for j in range(2):
                wait(("a", k, o, j), arecv.at[POS[k], o, j])
        wait(("a", 2, o), arecv.at[POS[2], o])
    wait(("a", 0, 1), arecv.at[0, 1])

    away = ((1, 1), (0, 1), (1, 0))
    for half in range(2):
        for n in range(half * COLS // 2, (half + 1) * COLS // 2, 384):
            r = jnp.zeros((4 * ROWS, 384), F32)
            for p in range(NX):
                left = arecv[p].reshape(4 * ROWS, NH * HD)
                r = r + jnp.dot(left, wo[p, :, n:n + 384], preferred_element_type=F32)
            part[:, :, :, n:n + 384] = r.astype(BF16).reshape(2, 2, ROWS, 384)
        columns = pl.ds(half * COLS // 2, COLS // 2)
        for o, j in away:
            where = device(y_hi=(y_hi + j) % 2, y_lo=(y_lo + o) % 2)
            send(("p", o, j, half), part.at[o, j, :, columns], precv.at[o, j, :, columns], where)
    for half in range(2):
        for o, j in away:
            wait(("p", o, j, half), precv.at[o, j, :, pl.ds(half * COLS // 2, COLS // 2)])
    out_ref[:, rows(1 - y_lo, COLS, COLS)] = (precv[1, 0].astype(F32) + precv[1, 1].astype(F32)).astype(BF16)
    out_ref[:, mine] = (part[0, 0].astype(F32) + precv[0, 1].astype(F32)).astype(BF16)

    for copy in pending:
        copy.wait_send()


def per_device(video_tokens, w_qkv, w_out, text_tokens, w_text, q_gain, k_gain, text_gain):
    vmem, hbm = pl.BlockSpec(memory_space=pltpu.VMEM), pl.BlockSpec(memory_space=pl.ANY)
    return pl.pallas_call(
        kernel,
        out_shape=jax.ShapeDtypeStruct((ROWS, D), BF16),
        in_specs=[hbm, hbm, hbm] + [vmem] * 5,
        out_specs=vmem,
        scratch_shapes=[
            pltpu.VMEM((2 * NX, ROWS, D), BF16),
            pltpu.VMEM((D, NH * 3 * HD), BF16),
            pltpu.VMEM((NX, NH * HD, COLS), BF16),
            pltpu.VMEM((2, NZ, 2 * NH, 2 * CHUNK, HD), BF16),
            pltpu.VMEM((NH, 4 * CHUNK, HD), BF16),
            pltpu.VMEM((NH, 4 * CHUNK, HD), F32),
            pltpu.VMEM((NH, 4 * CHUNK, HD), F32),
            pltpu.VMEM((NH, 4 * CHUNK, HD), F32),
            pltpu.VMEM((2, TEXT, NH * HD), F32),
            pltpu.VMEM((TEXT, NH * HD), F32),
            pltpu.VMEM((TEXT, NH * HD), F32),
            pltpu.VMEM((CHUNK, NH * HD), F32),
            pltpu.VMEM((CHUNK, NH * HD), F32),
            pltpu.VMEM((NZ - 1, HALF, NH * HD), F32),
            pltpu.VMEM((2 * NH, CHUNK, HD), BF16),
            pltpu.VMEM((2, CHUNK, NH * HD), BF16),
            pltpu.VMEM((2, CHUNK, NH * HD), BF16),
            pltpu.VMEM((2, 8, HD), F32),
            pltpu.VMEM((2, 8, HD), F32),
            pltpu.VMEM((NX, 2, ROWS, NH * HD), BF16),
            pltpu.VMEM((NX, 2, 2, ROWS, NH * HD), BF16),
            pltpu.VMEM((2, 2, ROWS, COLS), BF16),
            pltpu.VMEM((2, 2, ROWS, COLS), BF16),
            pltpu.SemaphoreType.DMA((N_SEMS,)),
            pltpu.SemaphoreType.DMA((N_SEMS,)),
            pltpu.SemaphoreType.DMA((3,)),
        ],
        compiler_params=pltpu.CompilerParams(
            collective_id=0, has_side_effects=True, vmem_limit_bytes=56 * 1024 * 1024
        ),
        name="joint_attention",
    )(
        video_tokens, w_qkv, w_out, text_tokens.T, w_text,
        q_gain.reshape(1, HD), k_gain.reshape(1, HD), text_gain.reshape(1, HD),
    )


def solution(mesh):
    in_specs = (
        P(("blk", "uly"), None), P(None, "uly"), P("uly", None), P(None, "blk"), P("blk", "uly"), P(), P(), P(),
    )
    return jax.shard_map(
        per_device, mesh=mesh, in_specs=in_specs, out_specs=P(("blk", "uly"), None), check_vma=False
    )
```

```python
import functools
import math

import jax
import jax.numpy as jnp
from jax import lax
from jax.experimental import pallas as pl
from jax.experimental.pallas import tpu as pltpu
from jax.sharding import PartitionSpec as P

MESH = pl.DeviceIdType.MESH
HD = 128
NH = 3
D = 3072
TEXT = 256
ROWS = 32
HALF = 16
CHUNK = 128
NZ, NX = 8, 4
COLS = D // 2
SHARE = NH * HD // 2
SLOTS = ((0, 0), (1, 0), (-1, 0), (0, 1), (2, 0), (1, 1), (-1, 1), (2, 1))
SLOT = {where: s for s, where in enumerate(SLOTS)}
POS = {0: 0, 1: 1, -1: 2, 2: 3}
GROUPS = ((0, 1), (1, 3), (4, 1), (5, 2), (7, 1))
SCALE2 = HD ** (-0.5) * math.log2(math.e)
BF16, F32 = jnp.bfloat16, jnp.float32


class Sems:
    def __init__(self, send, recv):
        self.send, self.recv, self.at = send, recv, {}

    def __call__(self, *name):
        index = self.at.setdefault(name, len(self.at))
        return {"send_sem": self.send.at[index], "recv_sem": self.recv.at[index]}


N_SEMS = 128


def normed(values, gains):
    factor = lax.rsqrt(jnp.mean(values * values, axis=-1, keepdims=True) + 1e-06)
    return values * factor * gains


def kernel(
    tok_hbm, wq_hbm, wo_hbm, tt_ref, wt_ref, qg_ref, kg_ref, tg_ref, out_ref,
    tok, wq, wo, kv, q, acc, top, total,
    tpart, tcr, tsum, tyr, tsum2, tzr, tkv,
    osend, orecv, ssend, srecv, att, arecv, part, precv,
    send_sems, recv_sems, local_sems,
):
    b, u = lax.axis_index("blk"), lax.axis_index("uly")
    y_lo, z, c = b // 16, (b // 2) % NZ, b % 2
    y_hi, x = u // NX, u % NX
    y = 2 * y_hi + y_lo
    sems = Sems(send_sems, recv_sems)
    pending = []

    def device(y_lo=y_lo, z=z, c=c, y_hi=y_hi, x=x):
        return {"blk": (y_lo * NZ + z) * 2 + c, "uly": y_hi * NX + x}

    def y_step(k):
        yy = (y + k) % 4
        return device(y_hi=yy // 2, y_lo=yy % 2)

    def x_step(k, o=0):
        return device(x=(x + k) % NX, y_lo=(y_lo + o) % 2)

    def z_step(k):
        return device(z=(z + k) % NZ)

    sibling = device(c=1 - c)
    partner = device(y_lo=1 - y_lo)

    def send(name, src, dst, where):
        copy = pltpu.make_async_remote_copy(
            src_ref=src, dst_ref=dst, device_id=where, device_id_type=MESH, **sems(*name)
        )
        copy.start()
        pending.append(copy)

    def wait(name, dst):
        pltpu.make_async_remote_copy(
            src_ref=dst, dst_ref=dst, device_id=sibling, device_id_type=MESH, **sems(*name)
        ).wait_recv()

    barrier = pltpu.get_barrier_semaphore()
    peers = [x_step(k, o) for k in (1, -1, 2) for o in range(2)]
    peers += [y_step(k) for k in (1, -1, 2)]
    peers += [z_step(k) for k in range(1, NZ)] + [sibling]
    for peer in peers:
        pl.semaphore_signal(barrier, inc=1, device_id=peer, device_id_type=MESH)

    def rows(start, size, step):
        return pl.ds(pl.multiple_of(start * step, step), size)

    def slot(dx, dy):
        return tok.at[SLOT[dx, dy]]

    mine = rows(y_lo, COLS, COLS)
    local_tok = pltpu.make_async_copy(tok_hbm, slot(0, 0), local_sems.at[0])
    local_wq = pltpu.make_async_copy(wq_hbm, wq, local_sems.at[1])
    local_wo = pltpu.make_async_copy(wo_hbm.at[:, mine], wo.at[0], local_sems.at[2])
    local_tok.start()
    local_wq.start()

    def kv_rows(g, core):
        first, count = GROUPS[g]
        return pl.ds(pl.multiple_of(core * CHUNK + first % 4 * ROWS, ROWS), count * ROWS)

    def project(g):
        first, count = GROUPS[g]
        j = first // 4

        @pl.loop(0, NH)
        def _(h):
            columns = pl.ds(pl.multiple_of(h * 3 * HD, HD), 3 * HD)
            left = tok[first:first + count].reshape(count * ROWS, D)
            r = jnp.dot(left, wq[:, columns], preferred_element_type=F32)
            q[h, first * ROWS:(first + count) * ROWS, :] = normed(r[:, :HD], qg_ref[...]).astype(BF16)
            kv[j, z, h, kv_rows(g, c), :] = normed(r[:, HD:2 * HD], kg_ref[...]).astype(BF16)
            kv[j, z, NH + h, kv_rows(g, c), :] = r[:, 2 * HD:].astype(BF16)

    def ring_start(g):
        block = kv.at[GROUPS[g][0] // 4, z, :, kv_rows(g, c), :]
        for k in (1, -1):
            send(("kv", g, k, 1), block, block, z_step(k))

    def finish_chunk(j):
        block = kv.at[j, z, :, rows(c, CHUNK, CHUNK), :]
        send(("sib", j, 0, 0), block, block, sibling)
        own, theirs = j * CHUNK, 2 * CHUNK + j * CHUNK
        send(("q", j), q.at[:, own:own + CHUNK, :], q.at[:, theirs:theirs + CHUNK, :], partner)

    def planes(h, k):
        if h < NZ // 2:
            return pl.ds(0, 2 * NH)
        return pl.ds(0 if k == 1 else NH, NH)

    def ring(g, h):
        j = GROUPS[g][0] // 4
        for k in (1, -1):
            zz = (z - k * h) % NZ
            wait(("kv", g, k, h), kv.at[j, zz, planes(h, k), kv_rows(g, c), :])
            if h < NZ // 2:
                piece = kv.at[j, zz, planes(h + 1, k), kv_rows(g, c), :]
                send(("kv", g, k, h + 1), piece, piece, z_step(k))

    def share(j, h):
        for k in (1, -1):
            piece = kv.at[j, (z - k * h) % NZ, planes(h, k), rows(c, CHUNK, CHUNK), :]
            send(("sib", j, h, k), piece, piece, sibling)

    def await_sibling(j, h):
        for k in (1, -1) if h else (0,):
            piece = planes(h, k) if h else pl.ds(0, 2 * NH)
            wait(("sib", j, h, k), kv.at[j, (z - k * h) % NZ, piece, rows(1 - c, CHUNK, CHUNK), :])

    def attend(tiles, first=0, size=4 * CHUNK):
        at = pl.ds(first, size)
        for h in range(NH):
            pairs = tiles(h)
            scores = []
            for keys, _ in pairs:
                s = lax.dot_general(q[h, at, :], keys[...], (((1,), (1,)), ((), ())), preferred_element_type=F32)
                scores.append([s[:, i:i + HD] for i in range(0, s.shape[1], HD)])
            peak = functools.reduce(jnp.maximum, [piece for s in scores for piece in s])
            old = top[h, at, :]
            new = jnp.maximum(old, jnp.max(peak, axis=1, keepdims=True))
            shrink = jnp.exp2((old - new) * SCALE2)
            weights = [[jnp.exp2((piece - new) * SCALE2) for piece in s] for s in scores]
            total[h, at, :] = total[h, at, :] * shrink + sum(piece for w in weights for piece in w)
            blended = acc[h, at, :] * shrink
            for w, (_, values) in zip(weights, pairs):
                w = jnp.concatenate(w, axis=1).astype(BF16)
                blended = blended + jnp.dot(w, values[...], preferred_element_type=F32)
            acc[h, at, :] = blended
            top[h, at, :] = new

    def video_tiles(*where):
        def tiles(h):
            return [(kv.at[j, zz, h], kv.at[j, zz, NH + h]) for j, zz in where]

        return tiles

    pl.semaphore_wait(barrier, len(peers))

    for k in (1, -1):
        send(("x", k), tok_hbm, slot(-k, 0), x_step(k))
    send(("y",), tok_hbm, slot(0, 1), y_step(2))

    product = lax.dot_general(tt_ref[...], wt_ref[...], (((0,), (0,)), ((), ())), preferred_element_type=F32)
    for h in range(NH):
        for s in range(2):
            at = (2 * h + s) * HD
            tpart[s, :, h * HD:(h + 1) * HD] = product[:, at:at + HD]
    send(("tc",), tpart.at[1 - c], tcr, sibling)
    local_tok.wait()
    local_wq.wait()
    local_wo.start()
    project(0)
    ring_start(0)
    send(("x", 2), tok_hbm, slot(2, 0), x_step(2))

    wait(("tc",), tcr)
    tsum[...] = tpart[c] + tcr[...]
    send(("ty",), tsum.at[rows(1 - y_lo, CHUNK, CHUNK), :], tyr, partner)

    wait(("y",), slot(0, 1))
    for k in (1, -1):
        send(("yx", k), slot(0, 1), slot(-k, 1), x_step(k))
    ring(0, 1)

    top[...] = jnp.full(top.shape, -1e30, F32)
    total[...] = jnp.zeros(total.shape, F32)
    acc[...] = jnp.zeros(acc.shape, F32)
    ssend[...] = jnp.zeros(ssend.shape, F32)

    for k in (1, -1):
        wait(("x", k), slot(-k, 0))
    project(1)
    ring_start(1)
    finish_chunk(0)
    ring(0, 2)

    wait(("ty",), tyr)
    tsum2[...] = tsum[rows(y_lo, CHUNK, CHUNK), :] + tyr[...]
    for dz in range(1, NZ):
        target = (z + dz) % NZ
        send(("tz", dz), tsum2.at[rows(target, HALF, HALF), :], tzr.at[dz - 1], z_step(dz))


    wait(("x", 2), slot(2, 0))
    send(("xy",), slot(2, 0), slot(2, 1), y_step(2))
    project(2)
    ring_start(2)

    ring(0, 3)
    ring(1, 1)
    share(0, 1)
    for k in (1, -1):
        wait(("yx", k), slot(-k, 1))

    project(3)
    ring_start(3)

    for k in (1, -1):
        here = rows(c, SHARE, SHARE)
        send(("w", k), wo_hbm.at[here, mine], wo.at[POS[-k], here, :], x_step(k))
    ring(0, 4)
    ring(2, 1)
    ring(1, 2)
    share(0, 2)

    wait(("xy",), slot(2, 1))
    project(4)
    ring_start(4)
    finish_chunk(1)

    ring(2, 2)

    for dz in range(1, NZ):
        wait(("tz", dz), tzr.at[dz - 1])
    summed = tsum2[rows(z, HALF, HALF), :]
    for dz in range(1, NZ):
        summed = summed + tzr[dz - 1]
    for h in range(NH):
        one = summed[:, h * HD:(h + 1) * HD]
        one = jnp.where(c == 0, normed(one, tg_ref[...]), one)
        tkv[c * NH + h, rows(z, HALF, HALF), :] = one.astype(BF16)

    def text_piece(dz):
        return tkv.at[pl.ds(c * NH, NH), rows((z - dz) % NZ, HALF, HALF), :]

    for dz in range(1, NZ):
        send(("tg", dz), text_piece(0), text_piece(0), z_step(dz))

    for j in range(2):
        theirs = 2 * CHUNK + j * CHUNK
        wait(("q", j), q.at[:, theirs:theirs + CHUNK, :])
    await_sibling(0, 0)
    await_sibling(1, 0)
    attend(video_tiles((0, z), (1, z)))

    def attend_far(j, h):
        await_sibling(j, h)
        attend(video_tiles((j, (z - h) % NZ), (j, (z + h) % NZ)))

    ring(3, 1)
    ring(4, 1)
    share(1, 1)
    attend_far(0, 1)
    ring(2, 3)
    ring(1, 3)
    share(0, 3)
    attend_far(0, 2)
    ring(3, 2)
    ring(4, 2)
    share(1, 2)
    attend_far(1, 1)
    ring(2, 4)
    ring(1, 4)
    share(0, 4)
    attend_far(0, 3)
    for dz in range(1, NZ):
        wait(("tg", dz), text_piece(dz))
    text_half = tkv.at[pl.ds(c * NH, NH), :, :]
    send(("ts",), text_half, text_half, sibling)

    def w_piece(dx, first=0, size=SHARE):
        return wo.at[POS[dx], pl.ds(pl.multiple_of(c * SHARE + first, SHARE // 2), size), :]

    for k, first in ((1, 0), (-1, SHARE // 2)):
        wait(("w", k), w_piece(-k))
        send(("ww", k), w_piece(-k, first, SHARE // 2), w_piece(2, first, SHARE // 2), x_step(k))
        send(("ws", -k), w_piece(-k), w_piece(-k), sibling)

    attend_far(1, 2)
    ring(3, 3)
    ring(4, 3)
    share(1, 3)
    wait(("ts",), tkv.at[pl.ds((1 - c) * NH, NH), :, :])
    attend(lambda h: [(tkv.at[h], tkv.at[NH + h])])
    await_sibling(0, 4)
    attend(video_tiles((0, (z + 4) % NZ)))
    attend_far(1, 3)
    ring(3, 4)
    ring(4, 4)
    share(1, 4)
    await_sibling(1, 4)
    last = video_tiles((1, (z + 4) % NZ))
    attend(last, 2 * CHUNK, 2 * CHUNK)

    def finished(h, at):
        weight = jnp.sum(total[h, at, :], axis=1, keepdims=True)
        return acc[h, at, :] / weight, top[h, at, :] * SCALE2 + jnp.log2(weight)

    for j in (1, 0):
        for h in range(NH):
            mean, level = finished(h, pl.ds(2 * CHUNK + j * CHUNK, CHUNK))
            osend[j, :, h * HD:(h + 1) * HD] = mean.astype(BF16)
            ssend[j, h:h + 1, :] = level.T[0:1, :]
        send(("s", j), ssend.at[j], srecv.at[j], partner)
        send(("o", j), osend.at[j], orecv.at[j], partner)

    attend(last, 0, 2 * CHUNK)

    while len(pending) > 4:
        pending.pop(0).wait_send()
    for k, first in ((1, 0), (-1, SHARE // 2)):
        wait(("ww", k), w_piece(2, first, SHARE // 2))
    send(("ws", 2), w_piece(2), w_piece(2), sibling)

    for j in (1, 0):
        wait(("s", j), srecv.at[j])
        wait(("o", j), orecv.at[j])
        for h in range(NH):
            mean, level = finished(h, pl.ds(j * CHUNK, CHUNK))
            other = jnp.broadcast_to(srecv[j, h:h + 1, :], (CHUNK, HD)).T
            peak = jnp.maximum(level, other)
            ours, theirs = jnp.exp2(level - peak), jnp.exp2(other - peak)
            both = mean * ours + orecv[j, :, h * HD:(h + 1) * HD].astype(F32) * theirs
            both = (both / (ours + theirs)).astype(BF16)
            for i in range(4):
                dx, dy = SLOTS[4 * j + i]
                att[POS[dx], dy, :, h * HD:(h + 1) * HD] = both[i * ROWS:(i + 1) * ROWS]

        for o in (1, 0):
            if j == 1:
                send(("a", 2, o), att.at[POS[2]], arecv.at[POS[2], o], x_step(2, o))
            for k in (1, -1):
                send(("a", -k, o, j), att.at[POS[k], j], arecv.at[POS[-k], o, j], x_step(k, o))
            if j == 0 and o == 1:
                send(("a", 0, o), att.at[0], arecv.at[0, o], partner)

    arecv[0, 0] = att[0]

    local_wo.wait()
    for dx in (1, -1, 2):
        wait(("ws", dx), wo.at[POS[dx], rows(1 - c, SHARE, SHARE), :])
    for o in range(2):
        for k in (1, -1):
            for j in range(2):
                wait(("a", k, o, j), arecv.at[POS[k], o, j])
        wait(("a", 2, o), arecv.at[POS[2], o])
    wait(("a", 0, 1), arecv.at[0, 1])

    away = ((1, 1), (0, 1), (1, 0))
    for half in range(2):
        for n in range(half * COLS // 2, (half + 1) * COLS // 2, 384):
            r = jnp.zeros((4 * ROWS, 384), F32)
            for p in range(NX):
                left = arecv[p].reshape(4 * ROWS, NH * HD)
                r = r + jnp.dot(left, wo[p, :, n:n + 384], preferred_element_type=F32)
            part[:, :, :, n:n + 384] = r.astype(BF16).reshape(2, 2, ROWS, 384)
        columns = pl.ds(half * COLS // 2, COLS // 2)
        for o, j in away:
            where = device(y_hi=(y_hi + j) % 2, y_lo=(y_lo + o) % 2)
            send(("p", o, j, half), part.at[o, j, :, columns], precv.at[o, j, :, columns], where)
    for half in range(2):
        for o, j in away:
            wait(("p", o, j, half), precv.at[o, j, :, pl.ds(half * COLS // 2, COLS // 2)])
    out_ref[:, rows(1 - y_lo, COLS, COLS)] = (precv[1, 0].astype(F32) + precv[1, 1].astype(F32)).astype(BF16)
    out_ref[:, mine] = (part[0, 0].astype(F32) + precv[0, 1].astype(F32)).astype(BF16)

    for copy in pending:
        copy.wait_send()


def per_device(video_tokens, w_qkv, w_out, text_tokens, w_text, q_gain, k_gain, text_gain):
    vmem, hbm = pl.BlockSpec(memory_space=pltpu.VMEM), pl.BlockSpec(memory_space=pl.ANY)
    return pl.pallas_call(
        kernel,
        out_shape=jax.ShapeDtypeStruct((ROWS, D), BF16),
        in_specs=[hbm, hbm, hbm] + [vmem] * 5,
        out_specs=vmem,
        scratch_shapes=[
            pltpu.VMEM((2 * NX, ROWS, D), BF16),
            pltpu.VMEM((D, NH * 3 * HD), BF16),
            pltpu.VMEM((NX, NH * HD, COLS), BF16),
            pltpu.VMEM((2, NZ, 2 * NH, 2 * CHUNK, HD), BF16),
            pltpu.VMEM((NH, 4 * CHUNK, HD), BF16),
            pltpu.VMEM((NH, 4 * CHUNK, HD), F32),
            pltpu.VMEM((NH, 4 * CHUNK, HD), F32),
            pltpu.VMEM((NH, 4 * CHUNK, HD), F32),
            pltpu.VMEM((2, TEXT, NH * HD), F32),
            pltpu.VMEM((TEXT, NH * HD), F32),
            pltpu.VMEM((TEXT, NH * HD), F32),
            pltpu.VMEM((CHUNK, NH * HD), F32),
            pltpu.VMEM((CHUNK, NH * HD), F32),
            pltpu.VMEM((NZ - 1, HALF, NH * HD), F32),
            pltpu.VMEM((2 * NH, CHUNK, HD), BF16),
            pltpu.VMEM((2, CHUNK, NH * HD), BF16),
            pltpu.VMEM((2, CHUNK, NH * HD), BF16),
            pltpu.VMEM((2, 8, HD), F32),
            pltpu.VMEM((2, 8, HD), F32),
            pltpu.VMEM((NX, 2, ROWS, NH * HD), BF16),
            pltpu.VMEM((NX, 2, 2, ROWS, NH * HD), BF16),
            pltpu.VMEM((2, 2, ROWS, COLS), BF16),
            pltpu.VMEM((2, 2, ROWS, COLS), BF16),
            pltpu.SemaphoreType.DMA((N_SEMS,)),
            pltpu.SemaphoreType.DMA((N_SEMS,)),
            pltpu.SemaphoreType.DMA((3,)),
        ],
        compiler_params=pltpu.CompilerParams(
            collective_id=0, has_side_effects=True, vmem_limit_bytes=56 * 1024 * 1024
        ),
        name="joint_attention",
    )(
        video_tokens, w_qkv, w_out, text_tokens.T, w_text,
        q_gain.reshape(1, HD), k_gain.reshape(1, HD), text_gain.reshape(1, HD),
    )


def solution(mesh):
    in_specs = (
        P(("blk", "uly"), None), P(None, "uly"), P("uly", None), P(None, "blk"), P("blk", "uly"), P(), P(), P(),
    )
    return jax.shard_map(
        per_device, mesh=mesh, in_specs=in_specs, out_specs=P(("blk", "uly"), None), check_vma=False
    )
```

```python
import functools
import math

import jax
import jax.numpy as jnp
from jax import lax
from jax.experimental import pallas as pl
from jax.experimental.pallas import tpu as pltpu
from jax.sharding import PartitionSpec as P

MESH = pl.DeviceIdType.MESH
HD = 128
NH = 3
D = 3072
TEXT = 256
ROWS = 32
HALF = 16
CHUNK = 128
NZ, NX = 8, 4
COLS = D // 2
SHARE = NH * HD // 2
SLOTS = ((0, 0), (1, 0), (-1, 0), (0, 1), (2, 0), (1, 1), (-1, 1), (2, 1))
SLOT = {where: s for s, where in enumerate(SLOTS)}
POS = {0: 0, 1: 1, -1: 2, 2: 3}
GROUPS = ((0, 1), (1, 3), (4, 1), (5, 2), (7, 1))
SCALE2 = HD ** (-0.5) * math.log2(math.e)
BF16, F32 = jnp.bfloat16, jnp.float32


class Sems:
    def __init__(self, send, recv):
        self.send, self.recv, self.at = send, recv, {}

    def __call__(self, *name):
        index = self.at.setdefault(name, len(self.at))
        return {"send_sem": self.send.at[index], "recv_sem": self.recv.at[index]}


N_SEMS = 128


def normed(values, gains):
    factor = lax.rsqrt(jnp.mean(values * values, axis=-1, keepdims=True) + 1e-06)
    return values * factor * gains


def kernel(
    tok_hbm, wq_hbm, wo_hbm, tt_ref, wt_ref, qg_ref, kg_ref, tg_ref, out_ref,
    tok, wq, wo, kv, q, acc, top, total,
    tpart, tcr, tsum, tyr, tsum2, tzr, tkv,
    osend, orecv, ssend, srecv, att, arecv, part, precv,
    send_sems, recv_sems, local_sems,
):
    b, u = lax.axis_index("blk"), lax.axis_index("uly")
    y_lo, z, c = b // 16, (b // 2) % NZ, b % 2
    y_hi, x = u // NX, u % NX
    y = 2 * y_hi + y_lo
    sems = Sems(send_sems, recv_sems)
    pending = []

    def device(y_lo=y_lo, z=z, c=c, y_hi=y_hi, x=x):
        return {"blk": (y_lo * NZ + z) * 2 + c, "uly": y_hi * NX + x}

    def y_step(k):
        yy = (y + k) % 4
        return device(y_hi=yy // 2, y_lo=yy % 2)

    def x_step(k, o=0):
        return device(x=(x + k) % NX, y_lo=(y_lo + o) % 2)

    def z_step(k):
        return device(z=(z + k) % NZ)

    sibling = device(c=1 - c)
    partner = device(y_lo=1 - y_lo)

    def send(name, src, dst, where):
        copy = pltpu.make_async_remote_copy(
            src_ref=src, dst_ref=dst, device_id=where, device_id_type=MESH, **sems(*name)
        )
        copy.start()
        pending.append(copy)

    def wait(name, dst):
        pltpu.make_async_remote_copy(
            src_ref=dst, dst_ref=dst, device_id=sibling, device_id_type=MESH, **sems(*name)
        ).wait_recv()

    barrier = pltpu.get_barrier_semaphore()
    peers = [x_step(k, o) for k in (1, -1, 2) for o in range(2)]
    peers += [y_step(k) for k in (1, -1, 2)]
    peers += [z_step(k) for k in range(1, NZ)] + [sibling]
    for peer in peers:
        pl.semaphore_signal(barrier, inc=1, device_id=peer, device_id_type=MESH)

    def rows(start, size, step):
        return pl.ds(pl.multiple_of(start * step, step), size)

    def slot(dx, dy):
        return tok.at[SLOT[dx, dy]]

    mine = rows(y_lo, COLS, COLS)
    local_tok = pltpu.make_async_copy(tok_hbm, slot(0, 0), local_sems.at[0])
    local_wq = pltpu.make_async_copy(wq_hbm, wq, local_sems.at[1])
    local_wo = pltpu.make_async_copy(wo_hbm.at[:, mine], wo.at[0], local_sems.at[2])
    local_tok.start()
    local_wq.start()

    def kv_rows(g, core):
        first, count = GROUPS[g]
        return pl.ds(pl.multiple_of(core * CHUNK + first % 4 * ROWS, ROWS), count * ROWS)

    def project(g):
        first, count = GROUPS[g]
        j = first // 4

        @pl.loop(0, NH)
        def _(h):
            columns = pl.ds(pl.multiple_of(h * 3 * HD, HD), 3 * HD)
            left = tok[first:first + count].reshape(count * ROWS, D)
            r = jnp.dot(left, wq[:, columns], preferred_element_type=F32)
            q[h, first * ROWS:(first + count) * ROWS, :] = normed(r[:, :HD], qg_ref[...]).astype(BF16)
            kv[j, z, h, kv_rows(g, c), :] = normed(r[:, HD:2 * HD], kg_ref[...]).astype(BF16)
            kv[j, z, NH + h, kv_rows(g, c), :] = r[:, 2 * HD:].astype(BF16)

    def ring_start(g):
        block = kv.at[GROUPS[g][0] // 4, z, :, kv_rows(g, c), :]
        for k in (1, -1):
            send(("kv", g, k, 1), block, block, z_step(k))

    def finish_chunk(j):
        block = kv.at[j, z, :, rows(c, CHUNK, CHUNK), :]
        send(("sib", j, 0, 0), block, block, sibling)
        own, theirs = j * CHUNK, 2 * CHUNK + j * CHUNK
        send(("q", j), q.at[:, own:own + CHUNK, :], q.at[:, theirs:theirs + CHUNK, :], partner)

    def planes(h, k):
        if h < NZ // 2:
            return pl.ds(0, 2 * NH)
        return pl.ds(0 if k == 1 else NH, NH)

    def ring(g, h):
        j = GROUPS[g][0] // 4
        for k in (1, -1):
            zz = (z - k * h) % NZ
            wait(("kv", g, k, h), kv.at[j, zz, planes(h, k), kv_rows(g, c), :])
            if h < NZ // 2:
                piece = kv.at[j, zz, planes(h + 1, k), kv_rows(g, c), :]
                send(("kv", g, k, h + 1), piece, piece, z_step(k))

    def share(j, h):
        for k in (1, -1):
            piece = kv.at[j, (z - k * h) % NZ, planes(h, k), rows(c, CHUNK, CHUNK), :]
            send(("sib", j, h, k), piece, piece, sibling)

    def await_sibling(j, h):
        for k in (1, -1) if h else (0,):
            piece = planes(h, k) if h else pl.ds(0, 2 * NH)
            wait(("sib", j, h, k), kv.at[j, (z - k * h) % NZ, piece, rows(1 - c, CHUNK, CHUNK), :])

    def attend(tiles, first=0, size=4 * CHUNK):
        at = pl.ds(first, size)
        for h in range(NH):
            pairs = tiles(h)
            scores = []
            for keys, _ in pairs:
                s = lax.dot_general(q[h, at, :], keys[...], (((1,), (1,)), ((), ())), preferred_element_type=F32)
                scores.append([s[:, i:i + HD] for i in range(0, s.shape[1], HD)])
            peak = functools.reduce(jnp.maximum, [piece for s in scores for piece in s])
            old = top[h, at, :]
            new = jnp.maximum(old, jnp.max(peak, axis=1, keepdims=True))
            shrink = jnp.exp2((old - new) * SCALE2)
            weights = [[jnp.exp2((piece - new) * SCALE2) for piece in s] for s in scores]
            total[h, at, :] = total[h, at, :] * shrink + sum(piece for w in weights for piece in w)
            blended = acc[h, at, :] * shrink
            for w, (_, values) in zip(weights, pairs):
                w = jnp.concatenate(w, axis=1).astype(BF16)
                blended = blended + jnp.dot(w, values[...], preferred_element_type=F32)
            acc[h, at, :] = blended
            top[h, at, :] = new

    def video_tiles(*where):
        def tiles(h):
            return [(kv.at[j, zz, h], kv.at[j, zz, NH + h]) for j, zz in where]

        return tiles

    pl.semaphore_wait(barrier, len(peers))

    for k in (1, -1):
        send(("x", k), tok_hbm, slot(-k, 0), x_step(k))
    send(("y",), tok_hbm, slot(0, 1), y_step(2))

    product = lax.dot_general(tt_ref[...], wt_ref[...], (((0,), (0,)), ((), ())), preferred_element_type=F32)
    for h in range(NH):
        for s in range(2):
            at = (2 * h + s) * HD
            tpart[s, :, h * HD:(h + 1) * HD] = product[:, at:at + HD]
    send(("tc",), tpart.at[1 - c], tcr, sibling)
    local_tok.wait()
    local_wq.wait()
    local_wo.start()
    project(0)
    ring_start(0)
    send(("x", 2), tok_hbm, slot(2, 0), x_step(2))

    wait(("tc",), tcr)
    tsum[...] = tpart[c] + tcr[...]
    send(("ty",), tsum.at[rows(1 - y_lo, CHUNK, CHUNK), :], tyr, partner)

    wait(("y",), slot(0, 1))
    for k in (1, -1):
        send(("yx", k), slot(0, 1), slot(-k, 1), x_step(k))
    ring(0, 1)

    top[...] = jnp.full(top.shape, -1e30, F32)
    total[...] = jnp.zeros(total.shape, F32)
    acc[...] = jnp.zeros(acc.shape, F32)
    ssend[...] = jnp.zeros(ssend.shape, F32)

    for k in (1, -1):
        wait(("x", k), slot(-k, 0))
    project(1)
    ring_start(1)
    finish_chunk(0)
    ring(0, 2)

    wait(("ty",), tyr)
    tsum2[...] = tsum[rows(y_lo, CHUNK, CHUNK), :] + tyr[...]
    for dz in range(1, NZ):
        target = (z + dz) % NZ
        send(("tz", dz), tsum2.at[rows(target, HALF, HALF), :], tzr.at[dz - 1], z_step(dz))


    wait(("x", 2), slot(2, 0))
    send(("xy",), slot(2, 0), slot(2, 1), y_step(2))
    project(2)
    ring_start(2)

    ring(0, 3)
    ring(1, 1)
    share(0, 1)
    for k in (1, -1):
        wait(("yx", k), slot(-k, 1))

    project(3)
    ring_start(3)

    for k in (1, -1):
        here = rows(c, SHARE, SHARE)
        send(("w", k), wo_hbm.at[here, mine], wo.at[POS[-k], here, :], x_step(k))
    ring(0, 4)
    ring(2, 1)
    ring(1, 2)
    ring(2, 2)
    share(0, 2)

    wait(("xy",), slot(2, 1))
    project(4)
    ring_start(4)
    finish_chunk(1)


    for dz in range(1, NZ):
        wait(("tz", dz), tzr.at[dz - 1])
    summed = tsum2[rows(z, HALF, HALF), :]
    for dz in range(1, NZ):
        summed = summed + tzr[dz - 1]
    for h in range(NH):
        one = summed[:, h * HD:(h + 1) * HD]
        one = jnp.where(c == 0, normed(one, tg_ref[...]), one)
        tkv[c * NH + h, rows(z, HALF, HALF), :] = one.astype(BF16)

    def text_piece(dz):
        return tkv.at[pl.ds(c * NH, NH), rows((z - dz) % NZ, HALF, HALF), :]

    for dz in range(1, NZ):
        send(("tg", dz), text_piece(0), text_piece(0), z_step(dz))

    for j in range(2):
        theirs = 2 * CHUNK + j * CHUNK
        wait(("q", j), q.at[:, theirs:theirs + CHUNK, :])
    await_sibling(0, 0)
    await_sibling(1, 0)
    attend(video_tiles((0, z), (1, z)))

    def attend_far(j, h):
        await_sibling(j, h)
        attend(video_tiles((j, (z - h) % NZ), (j, (z + h) % NZ)))

    ring(3, 1)
    ring(4, 1)
    share(1, 1)
    attend_far(0, 1)
    ring(2, 3)
    ring(1, 3)
    share(0, 3)
    attend_far(0, 2)
    ring(3, 2)
    ring(4, 2)
    share(1, 2)
    attend_far(1, 1)
    ring(2, 4)
    ring(1, 4)
    share(0, 4)
    attend_far(0, 3)
    for dz in range(1, NZ):
        wait(("tg", dz), text_piece(dz))
    text_half = tkv.at[pl.ds(c * NH, NH), :, :]
    send(("ts",), text_half, text_half, sibling)

    def w_piece(dx, first=0, size=SHARE):
        return wo.at[POS[dx], pl.ds(pl.multiple_of(c * SHARE + first, SHARE // 2), size), :]

    for k, first in ((1, 0), (-1, SHARE // 2)):
        wait(("w", k), w_piece(-k))
        send(("ww", k), w_piece(-k, first, SHARE // 2), w_piece(2, first, SHARE // 2), x_step(k))
        send(("ws", -k), w_piece(-k), w_piece(-k), sibling)

    attend_far(1, 2)
    ring(3, 3)
    ring(4, 3)
    share(1, 3)
    wait(("ts",), tkv.at[pl.ds((1 - c) * NH, NH), :, :])
    attend(lambda h: [(tkv.at[h], tkv.at[NH + h])])
    await_sibling(0, 4)
    attend(video_tiles((0, (z + 4) % NZ)))
    attend_far(1, 3)
    ring(3, 4)
    ring(4, 4)
    share(1, 4)
    await_sibling(1, 4)
    last = video_tiles((1, (z + 4) % NZ))
    attend(last, 2 * CHUNK, 2 * CHUNK)

    def finished(h, at):
        weight = jnp.sum(total[h, at, :], axis=1, keepdims=True)
        return acc[h, at, :] / weight, top[h, at, :] * SCALE2 + jnp.log2(weight)

    for j in (1, 0):
        for h in range(NH):
            mean, level = finished(h, pl.ds(2 * CHUNK + j * CHUNK, CHUNK))
            osend[j, :, h * HD:(h + 1) * HD] = mean.astype(BF16)
            ssend[j, h:h + 1, :] = level.T[0:1, :]
        send(("s", j), ssend.at[j], srecv.at[j], partner)
        send(("o", j), osend.at[j], orecv.at[j], partner)

    attend(last, 0, 2 * CHUNK)

    while len(pending) > 4:
        pending.pop(0).wait_send()
    for k, first in ((1, 0), (-1, SHARE // 2)):
        wait(("ww", k), w_piece(2, first, SHARE // 2))
    send(("ws", 2), w_piece(2), w_piece(2), sibling)

    for j in (1, 0):
        wait(("s", j), srecv.at[j])
        wait(("o", j), orecv.at[j])
        for h in range(NH):
            mean, level = finished(h, pl.ds(j * CHUNK, CHUNK))
            other = jnp.broadcast_to(srecv[j, h:h + 1, :], (CHUNK, HD)).T
            peak = jnp.maximum(level, other)
            ours, theirs = jnp.exp2(level - peak), jnp.exp2(other - peak)
            both = mean * ours + orecv[j, :, h * HD:(h + 1) * HD].astype(F32) * theirs
            both = (both / (ours + theirs)).astype(BF16)
            for i in range(4):
                dx, dy = SLOTS[4 * j + i]
                att[POS[dx], dy, :, h * HD:(h + 1) * HD] = both[i * ROWS:(i + 1) * ROWS]

        for o in (1, 0):
            if j == 1:
                send(("a", 2, o), att.at[POS[2]], arecv.at[POS[2], o], x_step(2, o))
            for k in (1, -1):
                send(("a", -k, o, j), att.at[POS[k], j], arecv.at[POS[-k], o, j], x_step(k, o))
            if j == 0 and o == 1:
                send(("a", 0, o), att.at[0], arecv.at[0, o], partner)

    arecv[0, 0] = att[0]

    local_wo.wait()
    for dx in (1, -1, 2):
        wait(("ws", dx), wo.at[POS[dx], rows(1 - c, SHARE, SHARE), :])
    for o in range(2):
        for k in (1, -1):
            for j in range(2):
                wait(("a", k, o, j), arecv.at[POS[k], o, j])
        wait(("a", 2, o), arecv.at[POS[2], o])
    wait(("a", 0, 1), arecv.at[0, 1])

    away = ((0, 1), (1, 1), (1, 0))
    for half in range(2):
        for n in range(half * COLS // 2, (half + 1) * COLS // 2, 384):
            r = jnp.zeros((4 * ROWS, 384), F32)
            for p in range(NX):
                left = arecv[p].reshape(4 * ROWS, NH * HD)
                r = r + jnp.dot(left, wo[p, :, n:n + 384], preferred_element_type=F32)
            part[:, :, :, n:n + 384] = r.astype(BF16).reshape(2, 2, ROWS, 384)
        columns = pl.ds(half * COLS // 2, COLS // 2)
        for o, j in away:
            where = device(y_hi=(y_hi + j) % 2, y_lo=(y_lo + o) % 2)
            send(("p", o, j, half), part.at[o, j, :, columns], precv.at[o, j, :, columns], where)
    for half in range(2):
        for o, j in away:
            wait(("p", o, j, half), precv.at[o, j, :, pl.ds(half * COLS // 2, COLS // 2)])
    out_ref[:, rows(1 - y_lo, COLS, COLS)] = (precv[1, 0].astype(F32) + precv[1, 1].astype(F32)).astype(BF16)
    out_ref[:, mine] = (part[0, 0].astype(F32) + precv[0, 1].astype(F32)).astype(BF16)

    for copy in pending:
        copy.wait_send()


def per_device(video_tokens, w_qkv, w_out, text_tokens, w_text, q_gain, k_gain, text_gain):
    vmem, hbm = pl.BlockSpec(memory_space=pltpu.VMEM), pl.BlockSpec(memory_space=pl.ANY)
    return pl.pallas_call(
        kernel,
        out_shape=jax.ShapeDtypeStruct((ROWS, D), BF16),
        in_specs=[hbm, hbm, hbm] + [vmem] * 5,
        out_specs=vmem,
        scratch_shapes=[
            pltpu.VMEM((2 * NX, ROWS, D), BF16),
            pltpu.VMEM((D, NH * 3 * HD), BF16),
            pltpu.VMEM((NX, NH * HD, COLS), BF16),
            pltpu.VMEM((2, NZ, 2 * NH, 2 * CHUNK, HD), BF16),
            pltpu.VMEM((NH, 4 * CHUNK, HD), BF16),
            pltpu.VMEM((NH, 4 * CHUNK, HD), F32),
            pltpu.VMEM((NH, 4 * CHUNK, HD), F32),
            pltpu.VMEM((NH, 4 * CHUNK, HD), F32),
            pltpu.VMEM((2, TEXT, NH * HD), F32),
            pltpu.VMEM((TEXT, NH * HD), F32),
            pltpu.VMEM((TEXT, NH * HD), F32),
            pltpu.VMEM((CHUNK, NH * HD), F32),
            pltpu.VMEM((CHUNK, NH * HD), F32),
            pltpu.VMEM((NZ - 1, HALF, NH * HD), F32),
            pltpu.VMEM((2 * NH, CHUNK, HD), BF16),
            pltpu.VMEM((2, CHUNK, NH * HD), BF16),
            pltpu.VMEM((2, CHUNK, NH * HD), BF16),
            pltpu.VMEM((2, 8, HD), F32),
            pltpu.VMEM((2, 8, HD), F32),
            pltpu.VMEM((NX, 2, ROWS, NH * HD), BF16),
            pltpu.VMEM((NX, 2, 2, ROWS, NH * HD), BF16),
            pltpu.VMEM((2, 2, ROWS, COLS), BF16),
            pltpu.VMEM((2, 2, ROWS, COLS), BF16),
            pltpu.SemaphoreType.DMA((N_SEMS,)),
            pltpu.SemaphoreType.DMA((N_SEMS,)),
            pltpu.SemaphoreType.DMA((3,)),
        ],
        compiler_params=pltpu.CompilerParams(
            collective_id=0, has_side_effects=True, vmem_limit_bytes=56 * 1024 * 1024
        ),
        name="joint_attention",
    )(
        video_tokens, w_qkv, w_out, text_tokens.T, w_text,
        q_gain.reshape(1, HD), k_gain.reshape(1, HD), text_gain.reshape(1, HD),
    )


def solution(mesh):
    in_specs = (
        P(("blk", "uly"), None), P(None, "uly"), P("uly", None), P(None, "blk"), P("blk", "uly"), P(), P(), P(),
    )
    return jax.shard_map(
        per_device, mesh=mesh, in_specs=in_specs, out_specs=P(("blk", "uly"), None), check_vma=False
    )
```
